512 devices in a mesh: seq: 64 (over y, x, core), head: 8 (over z).
Axes of the slice: x: 4, y: 8, z: 8, core: 2. Of those that a mesh axis runs over, the one named last changes fastest.
Arguments:
- stacked_keys: bfloat16 [196608, 4096], P('seq', 'head'), parts along dimension 1, may hold values from -6 to 6
- sketch: bfloat16 [512, 160], replicated, may hold values from -0.25 to 0.25
Outputs:
- basis: bfloat16 [196608, 1280], P('seq', 'head'), parts along dimension 1
- coefficients: float32 [1280, 512], P('head'), parts along dimension 0
The draws below stay inside these ranges and needn't reach their ends.
There are 8 independent parts, one for each index of `head`. The reference program is written for one: setup_inputs(seed, part) draws one part's arguments, and reference() takes and returns one part's arrays. A program takes and returns all parts, laid end to end along the dimension named above; an argument that names none is the same for every part. Nothing has to cross between parts.
All inputs are finite; a program needn't handle non-finite values.
Results may differ from the reference program's by a relative error of at most 0.001.
Values sent between devices are 32-bit elements; how exact they have to be, the bound alone decides.
No kernel may reach another device: no remote copies, remote signals or barrier semaphores. Data moves between devices by JAX's collectives and lax.ppermute only.
A program may use at most 64 MiB of HBM per device.

```python
import jax
import jax.numpy as jnp
from jax import lax

RANK = 160
KEY_COLS = 512
TOKENS = 196608


def block_levels(stream_key, extent, cuts, least, high):
    gain = 1.0
    for axis_at, shards_of in cuts:
        draws = jax.random.uniform(jax.random.fold_in(jax.random.fold_in(stream_key, 6), axis_at), (shards_of,), jnp.float32, least / len(cuts), high / len(cuts))
        gain = gain * jnp.repeat(jnp.exp(draws), extent[axis_at] // shards_of).reshape((-1,) + (1,) * (len(extent) - 1 - axis_at))
    return gain


def normal_values(key, dims, spread, limit, cuts=(), held_as=jnp.bfloat16):
    values = jax.random.normal(key, dims, jnp.float32) * spread
    if len(cuts) > 0:
        values = block_levels(key, dims, cuts, -0.22, 0.18) * values
    return jnp.clip(values, min=-limit, max=limit).astype(held_as)


def setup_inputs(seed: int = 0, part: int = 0) -> dict:
    arg_keys = jax.random.split(jax.random.key(seed), 3)
    part_keys = jax.random.split(jax.random.fold_in(arg_keys[2], part), 3)
    stacked_keys = normal_values(part_keys[0], (TOKENS, KEY_COLS), 1.0, 6.0, ((0, 64),))
    sketch = normal_values(arg_keys[1], (KEY_COLS, RANK), KEY_COLS ** -0.5, 0.25)
    return dict(stacked_keys=stacked_keys, sketch=sketch)


def reference(stacked_keys, sketch):
    sampled = jnp.dot(stacked_keys.astype(jnp.float32), sketch.astype(jnp.float32), preferred_element_type=jnp.float32)
    gram = jnp.dot(sampled.T, sampled, precision=lax.Precision.HIGHEST)
    lower = jnp.linalg.cholesky(gram)
    eye_mat = jnp.eye(gram.shape[0], dtype=gram.dtype)
    inverse = lax.linalg.triangular_solve(lower, eye_mat, left_side=True, lower=True)
    orthonormal = jnp.dot(sampled, inverse.T, precision=lax.Precision.HIGHEST)
    basis = (orthonormal * jnp.sqrt(jnp.float32(TOKENS))).astype(jnp.bfloat16)
    coefficients = jnp.dot(orthonormal.T, stacked_keys.astype(jnp.float32), precision=lax.Precision.HIGHEST)
    return (basis, coefficients)
```

```python
import functools

import jax
import jax.numpy as jnp
from jax import lax
from jax.experimental import pallas as pl
from jax.experimental.pallas import tpu as pltpu
from jax.sharding import Mesh, PartitionSpec as P

INNER = 16
ROWS_OUT, COLS_OUT = 40, 128
F32, BF16 = jnp.float32, jnp.bfloat16
MIB = 1 << 20


def dot(a, b, ca, cb):
    return lax.dot_general(a, b, (((ca,), (cb,)), ((), ())), preferred_element_type=F32)


def split3(x):
    a = x.astype(BF16)
    rest = x - a.astype(F32)
    b = rest.astype(BF16)
    return a, b, (rest - b.astype(F32)).astype(BF16)


def moments_kernel(k_ref, s_ref, m_ref, acc):
    step = pl.program_id(0)
    keys = k_ref[...]
    part = dot(keys, keys, 0, 0)

    @pl.when(step == 0)
    def _():
        acc[...] = part

    @pl.when(step > 0)
    def _():
        acc[...] += part

    @pl.when(step == pl.num_programs(0) - 1)
    def _():
        sketch = s_ref[...]
        total = jnp.zeros((sketch.shape[1], acc.shape[1]), F32)
        for piece in reversed(split3(acc[...])):
            total += dot(sketch, piece, 0, 0)
        put_chunks(m_ref, total)


def put_chunks(ref, m):
    wide = m.shape[1] // COLS_OUT
    for i in range(ref.shape[0]):
        r, c = i // wide * ROWS_OUT, i % wide * COLS_OUT
        ref[i] = m[r : r + ROWS_OUT, c : c + COLS_OUT]


def moments(keys, sketch, block=1024):
    tokens, cols = keys.shape
    rank = sketch.shape[1]
    chunks = (rank // ROWS_OUT) * (cols // COLS_OUT)
    return pl.pallas_call(
        moments_kernel,
        grid=(tokens // block,),
        out_shape=jax.ShapeDtypeStruct((chunks, ROWS_OUT, COLS_OUT), F32),
        in_specs=[
            pl.BlockSpec((block, cols), lambda i: (i, 0)),
            pl.BlockSpec((cols, rank), lambda i: (0, 0)),
        ],
        out_specs=pl.BlockSpec((chunks, ROWS_OUT, COLS_OUT), lambda i: (0, 0, 0)),
        scratch_shapes=[pltpu.VMEM((cols, cols), F32)],
        compiler_params=pltpu.CompilerParams(vmem_limit_bytes=24 * MIB),
        name="moments",
    )(keys, sketch)


def lanes_of(tile, j):
    return jnp.broadcast_to(tile[:, j : j + 1], (8, 128))


def row_of(tile, s):
    return jnp.broadcast_to(tile[s : s + 1, :], (8, 128))


def invert_factor(t):
    n, wide = len(t), len(t[0])
    sub = lax.broadcasted_iota(jnp.int32, (8, 128), 0)
    lane = lax.broadcasted_iota(jnp.int32, (8, 128), 1)
    for b in range(n):
        at, off = b // 16, 8 * (b % 16)
        cols = [lanes_of(t[b][at], off + s) for s in range(8)]
        solved, factor = list(t[b]), list(t[b])
        for s in range(8):
            here = sub == s
            pivot = row_of(cols[s], s)
            inv, root = 1.0 / pivot, lax.rsqrt(pivot)
            for h in range(wide):
                row, old = row_of(solved[h], s), solved[h]
                if h == at:
                    row = jnp.where(lane == off + s, 1.0, row)
                    old = jnp.where(lane == off + s, 0.0, old)
                factor[h] = jnp.where(here, row * root, factor[h])
                row = row * inv
                solved[h] = jnp.where(here, row, old - cols[s] * row)
            for k in range(s + 1, 8):
                val = row_of(cols[k], s) * inv
                cols[k] = jnp.where(here, val, cols[k] - cols[s] * val)
        in_block = (lane >= off) & (lane < off + 8)
        for i in range(b + 1, n):
            left = [lanes_of(t[i][at], off + s) for s in range(8)]
            for h in range(wide):
                x = t[i][h]
                if h == at:
                    x = jnp.where(in_block, 0.0, x)
                parts = [left[s] * row_of(solved[h], s) for s in range(8)]
                while len(parts) > 1:
                    parts = [p + q for p, q in zip(parts[::2], parts[1::2])]
                t[i][h] = x - parts[0]
        t[b] = factor
    return t


def basis_kernel(scale, block, m_ref, s_ref, k_hbm, q_hbm, c_ref, keys, out, tri, in_sem, out_sem):
    tokens, cols = keys.shape
    rank = s_ref.shape[1]
    steps = tokens // block
    load = pltpu.make_async_copy(k_hbm, keys, in_sem)
    load.start()
    sketch = s_ref[...]
    wide = cols // COLS_OUT
    m = jnp.concatenate(
        [
            jnp.concatenate([m_ref[r * wide + c] for c in range(wide)], axis=1)
            for r in range(rank // ROWS_OUT)
        ],
        axis=0,
    )
    pieces = split3(m)
    gram = jnp.zeros((rank, rank), F32)
    for piece in reversed(pieces):
        gram += dot(piece, sketch, 1, 0)
    tri[...] = jnp.zeros_like(tri)
    tri[:, :rank] = gram
    n, lanes = rank // 8, tri.shape[1] // 128
    t = [
        [tri[8 * i : 8 * i + 8, 128 * h : 128 * h + 128] for h in range(lanes)]
        for i in range(n)
    ]
    t = invert_factor(t)
    sub = lax.broadcasted_iota(jnp.int32, (8, 128), 0)
    lane = lax.broadcasted_iota(jnp.int32, (8, 128), 1)
    for i in range(n):
        for h in range(lanes):
            keep = lane + 128 * h <= sub + 8 * i
            tri[8 * i : 8 * i + 8, 128 * h : 128 * h + 128] = jnp.where(keep, t[i][h], 0.0)
    inverse = tri[:, :rank]
    a, b, c = split3(inverse)
    weights = scale * (dot(sketch, c, 1, 1) + dot(sketch, b, 1, 1) + dot(sketch, a, 1, 1))
    high = weights.astype(BF16)
    low = (weights - high.astype(F32)).astype(BF16)
    c_ref[...] = (
        dot(a, pieces[2], 1, 0) + dot(c, pieces[0], 1, 0) + dot(b, pieces[1], 1, 0)
        + dot(a, pieces[1], 1, 0) + dot(b, pieces[0], 1, 0) + dot(a, pieces[0], 1, 0)
    )
    load.wait()
    for i in range(steps):
        rows = pl.ds(i * block, block)
        x = keys[rows, :]
        out[rows, :] = (dot(x, low, 1, 0) + dot(x, high, 1, 0)).astype(BF16)
        pltpu.make_async_copy(out.at[rows, :], q_hbm.at[rows, :], out_sem.at[i]).start()
    for i in range(steps):
        rows = pl.ds(i * block, block)
        pltpu.make_async_copy(out.at[rows, :], q_hbm.at[rows, :], out_sem.at[i]).wait()


def finish(m, sketch, keys, total_tokens, block=512):
    tokens, cols = keys.shape
    rank = sketch.shape[1]
    vmem = pl.BlockSpec(memory_space=pltpu.VMEM)
    return pl.pallas_call(
        functools.partial(basis_kernel, float(total_tokens) ** 0.5, block),
        out_shape=(
            jax.ShapeDtypeStruct((tokens, rank), BF16),
            jax.ShapeDtypeStruct((rank, cols), F32),
        ),
        in_specs=[vmem, vmem, pl.BlockSpec(memory_space=pl.ANY)],
        out_specs=(pl.BlockSpec(memory_space=pl.ANY), vmem),
        scratch_shapes=[
            pltpu.VMEM((tokens, cols), BF16),
            pltpu.VMEM((tokens, rank), BF16),
            pltpu.VMEM((rank, -(-rank // 128) * 128), F32),
            pltpu.SemaphoreType.DMA,
            pltpu.SemaphoreType.DMA((tokens // block,)),
        ],
        compiler_params=pltpu.CompilerParams(vmem_limit_bytes=32 * MIB),
        name="basis",
    )(m, sketch, keys)


def spread(x, axis):
    n = lax.axis_size(axis)
    return lax.all_to_all(jnp.broadcast_to(x[None], (n,) + x.shape), axis, 0, 0)


def sum_over_seq(m):
    part = lax.all_to_all(m, "inner", 0, 0).sum(0)
    part = spread(part, "outer").sum(0)
    return spread(part, "inner")


def body(keys, sketch):
    total_tokens = keys.shape[0] * lax.axis_size("outer") * lax.axis_size("inner")
    m = sum_over_seq(moments(keys, sketch))
    return finish(m, sketch, keys, total_tokens)


def solution(mesh):
    seq, head = mesh.shape["seq"], mesh.shape["head"]
    devices = mesh.devices.reshape(seq // INNER, INNER, head)
    return jax.shard_map(
        body,
        mesh=Mesh(devices, ("outer", "inner", "head")),
        in_specs=(P(("outer", "inner"), "head"), P()),
        out_specs=(P(("outer", "inner"), "head"), P("head", None)),
        check_vma=False,
    )
```

```python
import functools

import jax
import jax.numpy as jnp
from jax import lax
from jax.experimental import pallas as pl
from jax.experimental.pallas import tpu as pltpu
from jax.sharding import Mesh, PartitionSpec as P

INNER = 16
ROWS_OUT, COLS_OUT = 40, 128
F32, BF16 = jnp.float32, jnp.bfloat16
MIB = 1 << 20


def dot(a, b, ca, cb):
    return lax.dot_general(a, b, (((ca,), (cb,)), ((), ())), preferred_element_type=F32)


def split3(x):
    a = x.astype(BF16)
    rest = x - a.astype(F32)
    b = rest.astype(BF16)
    return a, b, (rest - b.astype(F32)).astype(BF16)


def moments_kernel(block, k_hbm, st_hbm, m_ref, keys, st_ref, sem, st_sem):
    tokens, cols = keys.shape
    half = cols // 2
    copies = []
    for i in range(tokens // block):
        rows = pl.ds(i * block, block)
        copies.append(pltpu.make_async_copy(k_hbm.at[rows, :], keys.at[rows, :], sem.at[i]))
        copies[-1].start()
    st_copy = pltpu.make_async_copy(st_hbm, st_ref, st_sem)
    st_copy.start()
    top = jnp.zeros((half, cols), F32)
    low = jnp.zeros((half, half), F32)
    for i, copy in enumerate(copies):
        copy.wait()
        left = keys[i * block : (i + 1) * block, :half]
        right = keys[i * block : (i + 1) * block, half:]
        top += dot(left, keys[i * block : (i + 1) * block, :], 0, 0)
        low += dot(right, right, 0, 0)
    st_copy.wait()
    st = st_ref[...]
    first, second = st[:, :half], st[:, half:]
    m_left = jnp.zeros((st.shape[0], half), F32)
    m_right = jnp.zeros((st.shape[0], half), F32)
    for upper, lower in zip(reversed(split3(top)), reversed(split3(low))):
        m_left += dot(first, upper[:, :half], 1, 0) + dot(second, upper[:, half:], 1, 1)
        m_right += dot(first, upper[:, half:], 1, 0) + dot(second, lower, 1, 0)
    put_chunks(m_ref, jnp.concatenate([m_left, m_right], axis=1))


def put_chunks(ref, m):
    wide = m.shape[1] // COLS_OUT
    for i in range(ref.shape[0]):
        r, c = i // wide * ROWS_OUT, i % wide * COLS_OUT
        ref[i] = m[r : r + ROWS_OUT, c : c + COLS_OUT]


def in_hbm(x):
    return pltpu.with_memory_space_constraint(x, pltpu.HBM)


def moments(keys, sketch_t, block=768):
    tokens, cols = keys.shape
    rank = sketch_t.shape[0]
    chunks = (rank // ROWS_OUT) * (cols // COLS_OUT)
    vmem = pl.BlockSpec(memory_space=pltpu.VMEM)
    return pl.pallas_call(
        functools.partial(moments_kernel, block),
        out_shape=jax.ShapeDtypeStruct((chunks, ROWS_OUT, COLS_OUT), F32),
        in_specs=[pl.BlockSpec(memory_space=pltpu.HBM)] * 2,
        out_specs=vmem,
        scratch_shapes=[
            pltpu.VMEM((tokens, cols), BF16),
            pltpu.VMEM((rank, cols), BF16),
            pltpu.SemaphoreType.DMA((tokens // block,)),
            pltpu.SemaphoreType.DMA,
        ],
        compiler_params=pltpu.CompilerParams(vmem_limit_bytes=24 * MIB),
        name="moments",
    )(in_hbm(keys), in_hbm(sketch_t))


def lanes_of(tile, j):
    return jnp.broadcast_to(tile[:, j : j + 1], (8, 128))


def row_of(tile, s):
    return jnp.broadcast_to(tile[s : s + 1, :], (8, 128))


def invert_factor(t):
    n, wide = len(t), len(t[0])
    sub = lax.broadcasted_iota(jnp.int32, (8, 128), 0)
    lane = lax.broadcasted_iota(jnp.int32, (8, 128), 1)
    for b in range(n):
        at, off = b // 16, 8 * (b % 16)
        cols = [lanes_of(t[b][at], off + s) for s in range(8)]
        solved, factor = list(t[b]), list(t[b])
        for s in range(8):
            here = sub == s
            pivot = row_of(cols[s], s)
            inv, root = 1.0 / pivot, lax.rsqrt(pivot)
            for h in range(wide):
                row, old = row_of(solved[h], s), solved[h]
                if h == at:
                    row = jnp.where(lane == off + s, 1.0, row)
                    old = jnp.where(lane == off + s, 0.0, old)
                factor[h] = jnp.where(here, row * root, factor[h])
                row = row * inv
                solved[h] = jnp.where(here, row, old - cols[s] * row)
            for k in range(s + 1, 8):
                val = row_of(cols[k], s) * inv
                cols[k] = jnp.where(here, val, cols[k] - cols[s] * val)
        in_block = (lane >= off) & (lane < off + 8)
        for i in range(b + 1, n):
            left = [lanes_of(t[i][at], off + s) for s in range(8)]
            for h in range(wide):
                x = t[i][h]
                if h == at:
                    x = jnp.where(in_block, 0.0, x)
                parts = [left[s] * row_of(solved[h], s) for s in range(8)]
                while len(parts) > 1:
                    parts = [p + q for p, q in zip(parts[::2], parts[1::2])]
                t[i][h] = x - parts[0]
        t[b] = factor
    return t


def basis_kernel(
    scale, block, m_ref, st_hbm, k_hbm, qt_hbm, c_hbm, keys, st_ref, out, coef, tri, in_sem, st_sem, out_sem, c_sem
):
    tokens, cols = keys.shape
    rank = st_ref.shape[0]
    steps = tokens // block
    st_copy = pltpu.make_async_copy(st_hbm, st_ref, st_sem)
    st_copy.start()
    load = pltpu.make_async_copy(k_hbm, keys, in_sem)
    load.start()
    wide = cols // COLS_OUT
    m = jnp.concatenate(
        [
            jnp.concatenate([m_ref[r * wide + c] for c in range(wide)], axis=1)
            for r in range(rank // ROWS_OUT)
        ],
        axis=0,
    )
    pieces = split3(m)
    st_copy.wait()
    st = st_ref[...]
    gram = jnp.zeros((rank, rank), F32)
    for piece in reversed(pieces):
        gram += dot(piece, st, 1, 1)
    tri[...] = jnp.zeros_like(tri)
    tri[:, :rank] = gram
    n, lanes = rank // 8, tri.shape[1] // 128
    t = [
        [tri[8 * i : 8 * i + 8, 128 * h : 128 * h + 128] for h in range(lanes)]
        for i in range(n)
    ]
    t = invert_factor(t)
    sub = lax.broadcasted_iota(jnp.int32, (8, 128), 0)
    lane = lax.broadcasted_iota(jnp.int32, (8, 128), 1)
    for i in range(n):
        for h in range(lanes):
            keep = lane + 128 * h <= sub + 8 * i
            tri[8 * i : 8 * i + 8, 128 * h : 128 * h + 128] = jnp.where(keep, t[i][h], 0.0)
    a, b, c = split3(tri[:, :rank])
    weights = scale * (dot(c, st, 1, 0) + dot(b, st, 1, 0) + dot(a, st, 1, 0))
    high = weights.astype(BF16)
    low = (weights - high.astype(F32)).astype(BF16)
    both = jnp.concatenate([high, low], axis=0)
    coef[...] = (
        dot(a, pieces[2], 1, 0) + dot(c, pieces[0], 1, 0) + dot(b, pieces[1], 1, 0)
        + dot(a, pieces[1], 1, 0) + dot(b, pieces[0], 1, 0) + dot(a, pieces[0], 1, 0)
    )
    c_out = pltpu.make_async_copy(coef, c_hbm, c_sem)
    c_out.start()
    load.wait()
    copies = []
    for i in range(steps):
        rows = pl.ds(i * block, block)
        y = dot(both, keys[rows, :], 1, 1)
        out[:, rows] = (y[:rank] + y[rank:]).astype(BF16)
        copies.append(pltpu.make_async_copy(out.at[:, rows], qt_hbm.at[:, rows], out_sem.at[i]))
        copies[-1].start()
    c_out.wait()
    for copy in copies:
        copy.wait()


def finish(m, sketch_t, keys, total_tokens, block=512):
    tokens, cols = keys.shape
    rank = sketch_t.shape[0]
    vmem = pl.BlockSpec(memory_space=pltpu.VMEM)
    hbm = pl.BlockSpec(memory_space=pltpu.HBM)
    return pl.pallas_call(
        functools.partial(basis_kernel, float(total_tokens) ** 0.5, block),
        out_shape=(
            jax.ShapeDtypeStruct((rank, tokens), BF16),
            jax.ShapeDtypeStruct((rank, cols), F32),
        ),
        in_specs=[vmem, hbm, hbm],
        out_specs=(hbm, hbm),
        scratch_shapes=[
            pltpu.VMEM((tokens, cols), BF16),
            pltpu.VMEM((rank, cols), BF16),
            pltpu.VMEM((rank, tokens), BF16),
            pltpu.VMEM((rank, cols), F32),
            pltpu.VMEM((rank, -(-rank // 128) * 128), F32),
            pltpu.SemaphoreType.DMA,
            pltpu.SemaphoreType.DMA,
            pltpu.SemaphoreType.DMA((tokens // block,)),
            pltpu.SemaphoreType.DMA,
        ],
        compiler_params=pltpu.CompilerParams(vmem_limit_bytes=32 * MIB),
        name="basis",
    )(m, in_hbm(sketch_t), in_hbm(keys))


def spread(x, axis):
    n = lax.axis_size(axis)
    return lax.all_to_all(jnp.broadcast_to(x[None], (n,) + x.shape), axis, 0, 0)


def sum_over_seq(m):
    part = lax.all_to_all(m, "inner", 0, 0).sum(0)
    part = spread(part, "outer").sum(0)
    return spread(part, "inner")


def body(keys, sketch):
    total_tokens = keys.shape[0] * lax.axis_size("outer") * lax.axis_size("inner")
    m = sum_over_seq(moments(keys, sketch.T))
    basis_t, coefficients = finish(m, sketch.T, keys, total_tokens)
    return basis_t.T, coefficients


def solution(mesh):
    seq, head = mesh.shape["seq"], mesh.shape["head"]
    devices = mesh.devices.reshape(seq // INNER, INNER, head)
    return jax.shard_map(
        body,
        mesh=Mesh(devices, ("outer", "inner", "head")),
        in_specs=(P(("outer", "inner"), "head"), P()),
        out_specs=(P(("outer", "inner"), "head"), P("head", None)),
        check_vma=False,
    )
```

```python
import functools

import jax
import jax.numpy as jnp
from jax import lax
from jax.experimental import pallas as pl
from jax.experimental.pallas import tpu as pltpu
from jax.sharding import Mesh, PartitionSpec as P

INNER = 16
ROWS_OUT, COLS_OUT = 40, 128
F32, BF16 = jnp.float32, jnp.bfloat16
MIB = 1 << 20


def dot(a, b, ca, cb):
    return lax.dot_general(a, b, (((ca,), (cb,)), ((), ())), preferred_element_type=F32)


def split3(x):
    a = x.astype(BF16)
    rest = x - a.astype(F32)
    b = rest.astype(BF16)
    return a, b, (rest - b.astype(F32)).astype(BF16)


def moments_kernel(block, k_hbm, st_hbm, m_ref, keys, st_ref, sem, st_sem):
    tokens, cols = keys.shape
    half = cols // 2
    copies = []
    for i in range(tokens // block):
        rows = pl.ds(i * block, block)
        copies.append(pltpu.make_async_copy(k_hbm.at[rows, :], keys.at[rows, :], sem.at[i]))
    ahead = 2
    for copy in copies[:ahead]:
        copy.start()
    st_copy = pltpu.make_async_copy(st_hbm, st_ref, st_sem)
    top = jnp.zeros((half, cols), F32)
    low = jnp.zeros((half, half), F32)
    for i, copy in enumerate(copies):
        copy.wait()
        if i + ahead < len(copies):
            copies[i + ahead].start()
        if i == 0:
            st_copy.start()
        left = keys[i * block : (i + 1) * block, :half]
        right = keys[i * block : (i + 1) * block, half:]
        top += dot(left, keys[i * block : (i + 1) * block, :], 0, 0)
        low += dot(right, right, 0, 0)
    st_copy.wait()
    st = st_ref[...]
    first, second = st[:, :half], st[:, half:]
    m_left = jnp.zeros((st.shape[0], half), F32)
    m_right = jnp.zeros((st.shape[0], half), F32)
    for upper, lower in zip(reversed(split3(top)), reversed(split3(low))):
        m_left += dot(first, upper[:, :half], 1, 0) + dot(second, upper[:, half:], 1, 1)
        m_right += dot(first, upper[:, half:], 1, 0) + dot(second, lower, 1, 0)
    put_chunks(m_ref, jnp.concatenate([m_left, m_right], axis=1))


def put_chunks(ref, m):
    wide = m.shape[1] // COLS_OUT
    for i in range(ref.shape[0]):
        r, c = i // wide * ROWS_OUT, i % wide * COLS_OUT
        ref[i] = m[r : r + ROWS_OUT, c : c + COLS_OUT]


def in_hbm(x):
    return pltpu.with_memory_space_constraint(x, pltpu.HBM)


def moments(keys, sketch_t, block=1024):
    tokens, cols = keys.shape
    rank = sketch_t.shape[0]
    chunks = (rank // ROWS_OUT) * (cols // COLS_OUT)
    vmem = pl.BlockSpec(memory_space=pltpu.VMEM)
    return pl.pallas_call(
        functools.partial(moments_kernel, block),
        out_shape=jax.ShapeDtypeStruct((chunks, ROWS_OUT, COLS_OUT), F32),
        in_specs=[pl.BlockSpec(memory_space=pltpu.HBM)] * 2,
        out_specs=vmem,
        scratch_shapes=[
            pltpu.VMEM((tokens, cols), BF16),
            pltpu.VMEM((rank, cols), BF16),
            pltpu.SemaphoreType.DMA((tokens // block,)),
            pltpu.SemaphoreType.DMA,
        ],
        compiler_params=pltpu.CompilerParams(vmem_limit_bytes=24 * MIB),
        name="moments",
    )(in_hbm(keys), in_hbm(sketch_t))


def lanes_of(tile, j):
    return jnp.broadcast_to(tile[:, j : j + 1], (8, 128))


def row_of(tile, s):
    return jnp.broadcast_to(tile[s : s + 1, :], (8, 128))


def invert_factor(t, per=2, panel=4):
    n, wide, width = len(t), len(t[0]), 8 * per
    sub = lax.broadcasted_iota(jnp.int32, (8, 128), 0)
    lane = lax.broadcasted_iota(jnp.int32, (8, 128), 1)
    for b in range(0, n, per):
        at, off = 8 * b // 128, 8 * b % 128
        cols = [[lanes_of(t[b + r][at], off + s) for r in range(per)] for s in range(width)]
        solved = [list(t[b + r]) for r in range(per)]
        factor = [list(t[b + r]) for r in range(per)]
        for s in range(width):
            p, q = divmod(s, 8)
            here = sub == q
            pivot = row_of(cols[s][p], q)
            inv, root = 1.0 / pivot, lax.rsqrt(pivot)
            for h in range(wide):
                row, olds = row_of(solved[p][h], q), [solved[r][h] for r in range(per)]
                if h == at:
                    row = jnp.where(lane == off + s, 1.0, row)
                    olds = [jnp.where(lane == off + s, 0.0, x) for x in olds]
                factor[p][h] = jnp.where(here, row * root, factor[p][h])
                row = row * inv
                for r in range(per):
                    x = olds[r] - cols[s][r] * row
                    solved[r][h] = jnp.where(here, row, x) if r == p else x
            for k in range(s + 1, width):
                val = row_of(cols[k][p], q) * inv
                for r in range(per):
                    x = cols[k][r] - cols[s][r] * val
                    cols[k][r] = jnp.where(here, val, x) if r == p else x
        in_block = (lane >= off) & (lane < off + width)
        end = min(n, (b // panel + 1) * panel)
        for i in range(b + per, end):
            left = [lanes_of(t[i][at], off + s) for s in range(width)]
            for h in range(wide):
                x = jnp.where(in_block, 0.0, t[i][h]) if h == at else t[i][h]
                parts = [left[s] * row_of(solved[s // 8][h], s % 8) for s in range(width)]
                while len(parts) > 1:
                    parts = [p + q for p, q in zip(parts[::2], parts[1::2])]
                t[i][h] = x - parts[0]
        for r in range(per):
            t[b + r] = factor[r]
        if b + per == end and end < n:
            rows = range(end - panel, end)
            u = jnp.concatenate(
                [
                    jnp.concatenate(
                        [
                            jnp.where((lane + 128 * h > sub + 8 * i) & (lane + 128 * h < 8 * end), 0.0, t[i][h])
                            for h in range(wide)
                        ],
                        axis=1,
                    )
                    for i in rows
                ],
                axis=0,
            )
            a1, a2, a3 = split3(u)
            out = dot(
                jnp.concatenate([a3, a1, a2, a2, a1, a1], axis=0),
                jnp.concatenate([a1, a3, a2, a1, a2, a1], axis=0),
                0,
                0,
            )
            for i in range(end, n):
                for h in range(wide):
                    done = (lane + 128 * h >= 8 * (end - panel)) & (lane + 128 * h < 8 * end)
                    x = jnp.where(done, 0.0, t[i][h])
                    t[i][h] = x - out[8 * i : 8 * i + 8, 128 * h : 128 * h + 128]
    return t


def basis_kernel(
    scale, block, m_any, st_any, k_hbm, qt_hbm, c_hbm, m_ref, st_ref, keys, out, coef, tri, first_sem, in_sem, out_sem, c_sem
):
    tokens, cols = keys.shape
    rank = st_ref.shape[0]
    steps = tokens // block
    m_copy = pltpu.make_async_copy(m_any, m_ref, first_sem.at[0])
    st_copy = pltpu.make_async_copy(st_any, st_ref, first_sem.at[1])
    m_copy.start()
    st_copy.start()
    load = pltpu.make_async_copy(k_hbm, keys, in_sem)
    load.start()
    m_copy.wait()
    wide = cols // COLS_OUT
    m = jnp.concatenate(
        [
            jnp.concatenate([m_ref[r * wide + c] for c in range(wide)], axis=1)
            for r in range(rank // ROWS_OUT)
        ],
        axis=0,
    )
    pieces = split3(m)
    st_copy.wait()
    st = st_ref[...]
    gram = jnp.zeros((rank, rank), F32)
    for piece in reversed(pieces):
        gram += dot(piece, st, 1, 1)
    tri[...] = jnp.zeros_like(tri)
    tri[:, :rank] = gram
    n, lanes = rank // 8, tri.shape[1] // 128
    t = [
        [tri[8 * i : 8 * i + 8, 128 * h : 128 * h + 128] for h in range(lanes)]
        for i in range(n)
    ]
    t = invert_factor(t)
    sub = lax.broadcasted_iota(jnp.int32, (8, 128), 0)
    lane = lax.broadcasted_iota(jnp.int32, (8, 128), 1)
    for i in range(n):
        for h in range(lanes):
            keep = lane + 128 * h <= sub + 8 * i
            tri[8 * i : 8 * i + 8, 128 * h : 128 * h + 128] = jnp.where(keep, t[i][h], 0.0)
    a, b, c = split3(tri[:, :rank])
    weights = scale * (dot(c, st, 1, 0) + dot(b, st, 1, 0) + dot(a, st, 1, 0))
    high = weights.astype(BF16)
    low = (weights - high.astype(F32)).astype(BF16)
    both = jnp.concatenate([high, low], axis=0)
    coef[...] = (
        dot(a, pieces[2], 1, 0) + dot(c, pieces[0], 1, 0) + dot(b, pieces[1], 1, 0)
        + dot(a, pieces[1], 1, 0) + dot(b, pieces[0], 1, 0) + dot(a, pieces[0], 1, 0)
    )
    c_out = pltpu.make_async_copy(coef, c_hbm, c_sem)
    c_out.start()
    load.wait()
    copies = []
    for i in range(steps):
        rows = pl.ds(i * block, block)
        y = dot(both, keys[rows, :], 1, 1)
        out[:, rows] = (y[:rank] + y[rank:]).astype(BF16)
        copies.append(pltpu.make_async_copy(out.at[:, rows], qt_hbm.at[:, rows], out_sem.at[i]))
        copies[-1].start()
    c_out.wait()
    for copy in copies:
        copy.wait()


def finish(m, sketch_t, keys, total_tokens, block=512):
    tokens, cols = keys.shape
    rank = sketch_t.shape[0]
    anywhere = pl.BlockSpec(memory_space=pl.ANY)
    hbm = pl.BlockSpec(memory_space=pltpu.HBM)
    return pl.pallas_call(
        functools.partial(basis_kernel, float(total_tokens) ** 0.5, block),
        out_shape=(
            jax.ShapeDtypeStruct((rank, tokens), BF16),
            jax.ShapeDtypeStruct((rank, cols), F32),
        ),
        in_specs=[anywhere, anywhere, hbm],
        out_specs=(hbm, hbm),
        scratch_shapes=[
            pltpu.VMEM(m.shape, F32),
            pltpu.VMEM((rank, cols), BF16),
            pltpu.VMEM((tokens, cols), BF16),
            pltpu.VMEM((rank, tokens), BF16),
            pltpu.VMEM((rank, cols), F32),
            pltpu.VMEM((rank, -(-rank // 128) * 128), F32),
            pltpu.SemaphoreType.DMA((2,)),
            pltpu.SemaphoreType.DMA,
            pltpu.SemaphoreType.DMA((tokens // block,)),
            pltpu.SemaphoreType.DMA,
        ],
        compiler_params=pltpu.CompilerParams(vmem_limit_bytes=32 * MIB),
        name="basis",
    )(m, sketch_t, in_hbm(keys))


def spread(x, axis):
    n = lax.axis_size(axis)
    return lax.all_to_all(jnp.broadcast_to(x[None], (n,) + x.shape), axis, 0, 0)


def sum_over_seq(m):
    part = lax.all_to_all(m, "inner", 0, 0).sum(0)
    part = spread(part, "outer").sum(0)
    return spread(part, "inner")


def body(keys, sketch):
    total_tokens = keys.shape[0] * lax.axis_size("outer") * lax.axis_size("inner")
    m = sum_over_seq(moments(keys, sketch.T))
    basis_t, coefficients = finish(m, sketch.T, keys, total_tokens)
    return basis_t.T, coefficients


def solution(mesh):
    seq, head = mesh.shape["seq"], mesh.shape["head"]
    devices = mesh.devices.reshape(seq // INNER, INNER, head)
    return jax.shard_map(
        body,
        mesh=Mesh(devices, ("outer", "inner", "head")),
        in_specs=(P(("outer", "inner"), "head"), P()),
        out_specs=(P(("outer", "inner"), "head"), P("head", None)),
        check_vma=False,
    )
```

```python
import functools

import jax
import jax.numpy as jnp
from jax import lax
from jax.experimental import pallas as pl
from jax.experimental.pallas import tpu as pltpu
from jax.sharding import Mesh, PartitionSpec as P

INNER = 16
ROWS_OUT, COLS_OUT = 40, 128
FIRST = 3
F32, BF16 = jnp.float32, jnp.bfloat16
MIB = 1 << 20


def dot(a, b, ca, cb):
    return lax.dot_general(a, b, (((ca,), (cb,)), ((), ())), preferred_element_type=F32)


def split3(x):
    a = x.astype(BF16)
    rest = x - a.astype(F32)
    b = rest.astype(BF16)
    return a, b, (rest - b.astype(F32)).astype(BF16)


def moments_kernel(block, k_hbm, st_hbm, m_ref, keys, st_ref, sem, st_sem):
    tokens, cols = keys.shape
    copies = []
    for i in range(tokens // block):
        rows = pl.ds(i * block, block)
        copies.append(pltpu.make_async_copy(k_hbm.at[rows, :], keys.at[rows, :], sem.at[i]))
        copies[-1].start()
    st_copy = pltpu.make_async_copy(st_hbm, st_ref, st_sem)
    st_copy.start()
    both = jnp.zeros((cols, cols), F32)
    for i, copy in enumerate(copies):
        copy.wait()
        x = keys[i * block : (i + 1) * block, :]
        both += dot(x, x, 0, 0)
    st_copy.wait()
    st = st_ref[...]
    total = jnp.zeros((st.shape[0], cols), F32)
    for piece in reversed(split3(both)):
        total += dot(st, piece, 1, 0)
    put_chunks(m_ref, total)


def put_chunks(ref, m):
    wide = m.shape[1] // COLS_OUT
    for i in range(ref.shape[0]):
        r, c = i // wide * ROWS_OUT, i % wide * COLS_OUT
        ref[i] = m[r : r + ROWS_OUT, c : c + COLS_OUT]


def in_hbm(x):
    return pltpu.with_memory_space_constraint(x, pltpu.HBM)


def moments(keys, sketch_t, block=1024):
    tokens, cols = keys.shape
    rank = sketch_t.shape[0]
    chunks = (rank // ROWS_OUT) * (cols // COLS_OUT)
    vmem = pl.BlockSpec(memory_space=pltpu.VMEM)
    return pl.pallas_call(
        functools.partial(moments_kernel, block),
        out_shape=jax.ShapeDtypeStruct((chunks, ROWS_OUT, COLS_OUT), F32),
        in_specs=[pl.BlockSpec(memory_space=pltpu.HBM)] * 2,
        out_specs=vmem,
        scratch_shapes=[
            pltpu.VMEM((tokens, cols), BF16),
            pltpu.VMEM((rank, cols), BF16),
            pltpu.SemaphoreType.DMA((tokens // block,)),
            pltpu.SemaphoreType.DMA,
        ],
        compiler_params=pltpu.CompilerParams(vmem_limit_bytes=24 * MIB),
        name="moments",
    )(in_hbm(keys), in_hbm(sketch_t))


def lanes_of(tile, j):
    return jnp.broadcast_to(tile[:, j : j + 1], (8, 128))


def row_of(tile, s):
    return jnp.broadcast_to(tile[s : s + 1, :], (8, 128))


def invert_factor(t, per=2, panel=2, beside=lambda block: None):
    n, wide, width = len(t), len(t[0]), 8 * per
    sub = lax.broadcasted_iota(jnp.int32, (8, 128), 0)
    lane = lax.broadcasted_iota(jnp.int32, (8, 128), 1)
    for b in range(0, n, per):
        at, off = 8 * b // 128, 8 * b % 128
        cols = [[lanes_of(t[b + r][at], off + s) for r in range(per)] for s in range(width)]
        solved = [list(t[b + r]) for r in range(per)]
        factor = [list(t[b + r]) for r in range(per)]
        for s in range(width):
            p, q = divmod(s, 8)
            here = sub == q
            pivot = row_of(cols[s][p], q)
            inv, root = 1.0 / pivot, lax.rsqrt(pivot)
            for h in range(wide):
                row, olds = row_of(solved[p][h], q), [solved[r][h] for r in range(per)]
                if h == at:
                    row = jnp.where(lane == off + s, 1.0, row)
                    olds = [jnp.where(lane == off + s, 0.0, x) for x in olds]
                factor[p][h] = jnp.where(here, row * root, factor[p][h])
                row = row * inv
                for r in range(per):
                    x = olds[r] - cols[s][r] * row
                    solved[r][h] = jnp.where(here, row, x) if r == p else x
            for k in range(s + 1, width):
                val = row_of(cols[k][p], q) * inv
                for r in range(per):
                    x = cols[k][r] - cols[s][r] * val
                    cols[k][r] = jnp.where(here, val, x) if r == p else x
        in_block = (lane >= off) & (lane < off + width)
        end, far = (b // panel + 1) * panel, min(n, (b // panel + 2) * panel)
        for i in range(b + per, far):
            left = [lanes_of(t[i][at], off + s) for s in range(width)]
            for h in range(wide):
                x = jnp.where(in_block, 0.0, t[i][h]) if h == at else t[i][h]
                parts = [left[s] * row_of(solved[s // 8][h], s % 8) for s in range(width)]
                while len(parts) > 1:
                    parts = [p + q for p, q in zip(parts[::2], parts[1::2])]
                t[i][h] = x - parts[0]
        for r in range(per):
            t[b + r] = factor[r]
        beside(b // per)
        if b + per == end and far < n:
            rows = range(end - panel, end)
            u = jnp.concatenate(
                [
                    jnp.concatenate(
                        [
                            jnp.where((lane + 128 * h > sub + 8 * i) & (lane + 128 * h < 8 * end), 0.0, t[i][h])
                            for h in range(wide)
                        ],
                        axis=1,
                    )
                    for i in rows
                ],
                axis=0,
            )
            a1, a2, a3 = split3(u)
            skip = 8 * far // 128 * 128
            out = dot(
                jnp.concatenate([a3, a1, a2, a2, a1, a1], axis=0)[:, skip:],
                jnp.concatenate([a1, a3, a2, a1, a2, a1], axis=0),
                0,
                0,
            )
            for i in range(far, n):
                for h in range(wide):
                    done = (lane + 128 * h >= 8 * (end - panel)) & (lane + 128 * h < 8 * end)
                    x = jnp.where(done, 0.0, t[i][h])
                    t[i][h] = x - out[8 * i - skip : 8 * i + 8 - skip, 128 * h : 128 * h + 128]
    return t


def basis_kernel(
    scale, block, m_any, st_any, k_hbm, qt_hbm, c_hbm, m_ref, st_ref, keys, s_high, s_low, out, coef, tri, first_sem, in_sem, out_sem, c_sem
):
    tokens, cols = keys.shape
    rank = st_ref.shape[0]
    steps = tokens // block
    m_copy = pltpu.make_async_copy(m_any, m_ref, first_sem.at[0])
    st_copy = pltpu.make_async_copy(st_any, st_ref, first_sem.at[1])
    m_copy.start()
    st_copy.start()
    load = pltpu.make_async_copy(k_hbm, keys, in_sem)
    load.start()
    m_copy.wait()
    wide = cols // COLS_OUT
    m = jnp.concatenate(
        [
            jnp.concatenate([m_ref[r * wide + c] for c in range(wide)], axis=1)
            for r in range(rank // ROWS_OUT)
        ],
        axis=0,
    )
    pieces = split3(m)
    st_copy.wait()
    st = st_ref[...]
    gram = jnp.zeros((rank, rank), F32)
    for piece in reversed(pieces):
        gram += dot(piece, st, 1, 1)
    tri[...] = jnp.zeros_like(tri)
    tri[:, :rank] = gram
    n, lanes = rank // 8, tri.shape[1] // 128
    t = [
        [tri[8 * i : 8 * i + 8, 128 * h : 128 * h + 128] for h in range(lanes)]
        for i in range(n)
    ]

    def sample(step):
        if step == FIRST:
            load.wait()
        i = step - FIRST
        if 0 <= i < steps:
            rows = pl.ds(i * block, block)
            y = dot(st, keys[rows, :], 1, 1)
            high = y.astype(BF16)
            s_high[:, rows] = high
            s_low[:, rows] = (y - high.astype(F32)).astype(BF16)

    t = invert_factor(t, beside=sample)
    sub = lax.broadcasted_iota(jnp.int32, (8, 128), 0)
    lane = lax.broadcasted_iota(jnp.int32, (8, 128), 1)
    for i in range(n):
        for h in range(lanes):
            keep = lane + 128 * h <= sub + 8 * i
            tri[8 * i : 8 * i + 8, 128 * h : 128 * h + 128] = jnp.where(keep, t[i][h], 0.0)
    a, b, c = split3(tri[:, :rank])
    scaled = scale * tri[:, :rank]
    high = scaled.astype(BF16)
    low = (scaled - high.astype(F32)).astype(BF16)
    both = jnp.concatenate([high, low], axis=0)
    coef[...] = dot(a, pieces[1], 1, 0) + dot(b, pieces[0], 1, 0) + dot(a, pieces[0], 1, 0)
    c_out = pltpu.make_async_copy(coef, c_hbm, c_sem)
    c_out.start()
    copies = []
    for i in range(steps):
        rows = pl.ds(i * block, block)
        y = dot(both, s_high[:, rows], 1, 0)
        y = y[:rank] + (y[rank:] + dot(high, s_low[:, rows], 1, 0))
        out[:, rows] = y.astype(BF16)
        copies.append(pltpu.make_async_copy(out.at[:, rows], qt_hbm.at[:, rows], out_sem.at[i]))
        copies[-1].start()
    c_out.wait()
    for copy in copies:
        copy.wait()


def finish(m, sketch_t, keys, total_tokens, block=512):
    tokens, cols = keys.shape
    rank = sketch_t.shape[0]
    anywhere = pl.BlockSpec(memory_space=pl.ANY)
    hbm = pl.BlockSpec(memory_space=pltpu.HBM)
    return pl.pallas_call(
        functools.partial(basis_kernel, float(total_tokens) ** 0.5, block),
        out_shape=(
            jax.ShapeDtypeStruct((rank, tokens), BF16),
            jax.ShapeDtypeStruct((rank, cols), F32),
        ),
        in_specs=[anywhere, anywhere, hbm],
        out_specs=(hbm, hbm),
        scratch_shapes=[
            pltpu.VMEM(m.shape, F32),
            pltpu.VMEM((rank, cols), BF16),
            pltpu.VMEM((tokens, cols), BF16),
            pltpu.VMEM((rank, tokens), BF16),
            pltpu.VMEM((rank, tokens), BF16),
            pltpu.VMEM((rank, tokens), BF16),
            pltpu.VMEM((rank, cols), F32),
            pltpu.VMEM((rank, -(-rank // 128) * 128), F32),
            pltpu.SemaphoreType.DMA((2,)),
            pltpu.SemaphoreType.DMA,
            pltpu.SemaphoreType.DMA((tokens // block,)),
            pltpu.SemaphoreType.DMA,
        ],
        compiler_params=pltpu.CompilerParams(vmem_limit_bytes=32 * MIB),
        name="basis",
    )(m, sketch_t, in_hbm(keys))


def spread(x, axis):
    n = lax.axis_size(axis)
    return lax.all_to_all(jnp.broadcast_to(x[None], (n,) + x.shape), axis, 0, 0)


def sum_over_seq(m):
    part = lax.all_to_all(m, "inner", 0, 0).sum(0)
    part = spread(part, "outer").sum(0)
    return spread(part, "inner")


def body(keys, sketch):
    total_tokens = keys.shape[0] * lax.axis_size("outer") * lax.axis_size("inner")
    m = sum_over_seq(moments(keys, sketch.T))
    basis_t, coefficients = finish(m, sketch.T, keys, total_tokens)
    return basis_t.T, coefficients


def solution(mesh):
    seq, head = mesh.shape["seq"], mesh.shape["head"]
    devices = mesh.devices.reshape(seq // INNER, INNER, head)
    return jax.shard_map(
        body,
        mesh=Mesh(devices, ("outer", "inner", "head")),
        in_specs=(P(("outer", "inner"), "head"), P()),
        out_specs=(P(("outer", "inner"), "head"), P("head", None)),
        check_vma=False,
    )
```

```python
import functools

import jax
import jax.numpy as jnp
from jax import lax
from jax.experimental import pallas as pl
from jax.experimental.pallas import tpu as pltpu
from jax.sharding import Mesh, PartitionSpec as P

INNER = 16
ROWS_OUT, COLS_OUT = 40, 128
AHEAD = 1
FIRST = 3
F32, BF16 = jnp.float32, jnp.bfloat16
MIB = 1 << 20


def dot(a, b, ca, cb):
    return lax.dot_general(a, b, (((ca,), (cb,)), ((), ())), preferred_element_type=F32)


def split3(x):
    a = x.astype(BF16)
    rest = x - a.astype(F32)
    b = rest.astype(BF16)
    return a, b, (rest - b.astype(F32)).astype(BF16)


def moments_kernel(block, k_hbm, st_hbm, m_ref, keys, st_ref, sem, st_sem):
    tokens, cols = keys.shape
    h = cols // 2
    copies = []
    for i in range(tokens // block):
        rows = pl.ds(i * block, block)
        copies.append(pltpu.make_async_copy(k_hbm.at[rows, :], keys.at[rows, :], sem.at[i]))
        copies[-1].start()
    st_copy = pltpu.make_async_copy(st_hbm, st_ref, st_sem)
    st_copy.start()
    top = jnp.zeros((h, cols), F32)
    low = jnp.zeros((h, h), F32)
    for i, copy in enumerate(copies):
        copy.wait()
        x = keys[i * block : (i + 1) * block, :]
        r = x[:, h:]
        top += dot(x[:, :h], x, 0, 0)
        low += jnp.concatenate([dot(r[:, : h // 2], r, 0, 0), dot(r[:, h // 2 :], r, 0, 0)], axis=0)
    st_copy.wait()
    st = st_ref[...]
    tops, lows = split3(top)[::-1], split3(low)[::-1]
    first = jnp.concatenate([st[:, :h]] * 3, axis=1)
    second = jnp.concatenate([st[:, h:]] * 3, axis=1)
    corner = jnp.concatenate([x[:, :h] for x in tops], axis=0)
    upper = jnp.concatenate([x[:, h:] for x in tops], axis=0)
    lower_t = jnp.concatenate([x[:, h:] for x in tops], axis=1)
    left = dot(first, corner, 1, 0) + dot(second, lower_t, 1, 1)
    right = dot(first, upper, 1, 0) + dot(second, jnp.concatenate(lows, axis=0), 1, 0)
    put_chunks(m_ref, jnp.concatenate([left, right], axis=1))


def put_chunks(ref, m):
    wide = m.shape[1] // COLS_OUT
    for i in range(ref.shape[0]):
        r, c = i // wide * ROWS_OUT, i % wide * COLS_OUT
        ref[i] = m[r : r + ROWS_OUT, c : c + COLS_OUT]


def in_hbm(x):
    return pltpu.with_memory_space_constraint(x, pltpu.HBM)


def moments(keys, sketch_t, block=768):
    tokens, cols = keys.shape
    rank = sketch_t.shape[0]
    chunks = (rank // ROWS_OUT) * (cols // COLS_OUT)
    vmem = pl.BlockSpec(memory_space=pltpu.VMEM)
    return pl.pallas_call(
        functools.partial(moments_kernel, block),
        out_shape=jax.ShapeDtypeStruct((chunks, ROWS_OUT, COLS_OUT), F32),
        in_specs=[pl.BlockSpec(memory_space=pltpu.HBM)] * 2,
        out_specs=vmem,
        scratch_shapes=[
            pltpu.VMEM((tokens, cols), BF16),
            pltpu.VMEM((rank, cols), BF16),
            pltpu.SemaphoreType.DMA((tokens // block,)),
            pltpu.SemaphoreType.DMA,
        ],
        compiler_params=pltpu.CompilerParams(vmem_limit_bytes=24 * MIB),
        name="moments",
    )(in_hbm(keys), in_hbm(sketch_t))


def lanes_of(tile, j):
    return jnp.broadcast_to(tile[:, j : j + 1], (8, 128))


def row_of(tile, s):
    return jnp.broadcast_to(tile[s : s + 1, :], (8, 128))


def invert_factor(t, per=2, panel=2, beside=lambda block, t: None):
    n, wide, width = len(t), len(t[0]), 8 * per
    sub = lax.broadcasted_iota(jnp.int32, (8, 128), 0)
    lane = lax.broadcasted_iota(jnp.int32, (8, 128), 1)
    for b in range(0, n, per):
        at, off = 8 * b // 128, 8 * b % 128
        cols = [[lanes_of(t[b + r][at], off + s) for r in range(per)] for s in range(width)]
        solved = [list(t[b + r]) for r in range(per)]
        factor = [list(t[b + r]) for r in range(per)]
        for s in range(width):
            p, q = divmod(s, 8)
            here = sub == q
            pivot = row_of(cols[s][p], q)
            inv, root = 1.0 / pivot, lax.rsqrt(pivot)
            for h in range(wide):
                row, olds = row_of(solved[p][h], q), [solved[r][h] for r in range(per)]
                if h == at:
                    row = jnp.where(lane == off + s, 1.0, row)
                    olds = [jnp.where(lane == off + s, 0.0, x) for x in olds]
                factor[p][h] = jnp.where(here, row * root, factor[p][h])
                row = row * inv
                for r in range(per):
                    x = olds[r] - cols[s][r] * row
                    solved[r][h] = jnp.where(here, row, x) if r == p else x
            for k in range(s + 1, width):
                val = row_of(cols[k][p], q) * inv
                for r in range(per):
                    x = cols[k][r] - cols[s][r] * val
                    cols[k][r] = jnp.where(here, val, x) if r == p else x
        in_block = (lane >= off) & (lane < off + width)
        end, far = (b // panel + 1) * panel, min(n, (b // panel + 2) * panel)
        for i in range(b + per, far):
            left = [lanes_of(t[i][at], off + s) for s in range(width)]
            for h in range(wide):
                x = jnp.where(in_block, 0.0, t[i][h]) if h == at else t[i][h]
                parts = [left[s] * row_of(solved[s // 8][h], s % 8) for s in range(width)]
                while len(parts) > 1:
                    parts = [p + q for p, q in zip(parts[::2], parts[1::2])]
                t[i][h] = x - parts[0]
        for r in range(per):
            t[b + r] = factor[r]
        beside(b // per, t)
        if b + per == end and far < n:
            rows = range(end - panel, end)
            u = jnp.concatenate(
                [
                    jnp.concatenate(
                        [
                            jnp.where((lane + 128 * h > sub + 8 * i) & (lane + 128 * h < 8 * end), 0.0, t[i][h])
                            for h in range(wide)
                        ],
                        axis=1,
                    )
                    for i in rows
                ],
                axis=0,
            )
            a1, a2, a3 = split3(u)
            skip = 8 * far // 128 * 128
            out = dot(
                jnp.concatenate([a3, a1, a2, a2, a1, a1], axis=0)[:, skip:],
                jnp.concatenate([a1, a3, a2, a1, a2, a1], axis=0),
                0,
                0,
            )
            for i in range(far, n):
                for h in range(wide):
                    done = (lane + 128 * h >= 8 * (end - panel)) & (lane + 128 * h < 8 * end)
                    x = jnp.where(done, 0.0, t[i][h])
                    t[i][h] = x - out[8 * i - skip : 8 * i + 8 - skip, 128 * h : 128 * h + 128]
    return t


def basis_kernel(
    scale, block, m_any, st_any, k_hbm, qt_hbm, c_hbm, m_ref, st_ref, keys, s_high, s_low, out, coef, tri, first_sem, in_sem, out_sem
):
    tokens, cols = keys.shape
    rank = st_ref.shape[0]
    steps = tokens // block
    m_copy = pltpu.make_async_copy(m_any, m_ref, first_sem.at[0])
    st_copy = pltpu.make_async_copy(st_any, st_ref, first_sem.at[1])
    m_copy.start()
    st_copy.start()
    load = pltpu.make_async_copy(k_hbm, keys, in_sem)
    load.start()
    m_copy.wait()
    wide = cols // COLS_OUT
    m = jnp.concatenate(
        [
            jnp.concatenate([m_ref[r * wide + c] for c in range(wide)], axis=1)
            for r in range(rank // ROWS_OUT)
        ],
        axis=0,
    )
    pieces = split3(m)
    st_copy.wait()
    st = st_ref[...]
    gram = jnp.zeros((rank, rank), F32)
    for piece in reversed(pieces):
        gram += dot(piece, st, 1, 1)
    tri[...] = jnp.zeros_like(tri)
    tri[:, :rank] = gram
    n, lanes = rank // 8, tri.shape[1] // 128
    t = [
        [tri[8 * i : 8 * i + 8, 128 * h : 128 * h + 128] for h in range(lanes)]
        for i in range(n)
    ]

    def halves(x):
        high = x.astype(BF16)
        return high, (x - high.astype(F32)).astype(BF16)

    def lower(i, h):
        sub = lax.broadcasted_iota(jnp.int32, (8, 128), 0)
        lane = lax.broadcasted_iota(jnp.int32, (8, 128), 1)
        return jnp.where(lane + 128 * h <= sub + 8 * i, t[i][h], 0.0)

    copies = []

    def send(first, last, rows):
        piece = (pl.ds(first, last - first), rows)
        copies.append(pltpu.make_async_copy(out.at[piece], qt_hbm.at[piece], out_sem.at[len(copies)]))
        copies[-1].start()

    def basis_rows(first, last, x, chunk):
        depth, count = x.shape[1], last - first
        high, low = halves(scale * x)
        rows = pl.ds(chunk * block, block)
        y = dot(jnp.concatenate([high, low], axis=0), s_high[:depth, rows], 1, 0)
        y = y[:count] + (y[count:] + dot(high, s_low[:depth, rows], 1, 0))
        out[first:last, rows] = y.astype(BF16)
        send(first, last, rows)

    def coefficient_rows(first, last, x):
        depth = x.shape[1]
        high, low = halves(x)
        p = [piece[:depth] for piece in pieces[:2]]
        coef[first:last, :] = dot(high, p[1], 1, 0) + dot(low, p[0], 1, 0) + dot(high, p[0], 1, 0)
        piece = (pl.ds(first, last - first), slice(None))
        copies.append(pltpu.make_async_copy(coef.at[piece], c_hbm.at[piece], out_sem.at[len(copies)]))
        copies[-1].start()

    early = rank // 128 * 128
    ready = early // 16 - 1

    def beside(step, t):
        if step == FIRST:
            load.wait()
        i = step - FIRST
        if 0 <= i < steps:
            rows = pl.ds(i * block, block)
            y = dot(st, keys[rows, :], 1, 1)
            s_high[:, rows], s_low[:, rows] = halves(y)
        if step >= ready:
            x = jnp.concatenate(
                [jnp.concatenate([lower(i, h) for h in range(early // 128)], axis=1) for i in range(early // 8)],
                axis=0,
            )
            for chunk in range(steps):
                if (chunk < AHEAD) == (step == ready) and step <= ready + 1:
                    basis_rows(0, early, x, chunk)
            if step == ready + 1:
                coefficient_rows(0, early, x)

    t = invert_factor(t, beside=beside)
    for i in range(early // 8, n):
        for h in range(lanes):
            tri[8 * i : 8 * i + 8, 128 * h : 128 * h + 128] = lower(i, h)
    x = tri[early:, :rank]
    coefficient_rows(early, rank, x)
    for chunk in range(steps):
        basis_rows(early, rank, x, chunk)
    for copy in copies:
        copy.wait()


def finish(m, sketch_t, keys, total_tokens, block=1024):
    tokens, cols = keys.shape
    rank = sketch_t.shape[0]
    anywhere = pl.BlockSpec(memory_space=pl.ANY)
    hbm = pl.BlockSpec(memory_space=pltpu.HBM)
    return pl.pallas_call(
        functools.partial(basis_kernel, float(total_tokens) ** 0.5, block),
        out_shape=(
            jax.ShapeDtypeStruct((rank, tokens), BF16),
            jax.ShapeDtypeStruct((rank, cols), F32),
        ),
        in_specs=[anywhere, anywhere, hbm],
        out_specs=(hbm, hbm),
        scratch_shapes=[
            pltpu.VMEM(m.shape, F32),
            pltpu.VMEM((rank, cols), BF16),
            pltpu.VMEM((tokens, cols), BF16),
            pltpu.VMEM((rank, tokens), BF16),
            pltpu.VMEM((rank, tokens), BF16),
            pltpu.VMEM((rank, tokens), BF16),
            pltpu.VMEM((rank, cols), F32),
            pltpu.VMEM((rank, -(-rank // 128) * 128), F32),
            pltpu.SemaphoreType.DMA((2,)),
            pltpu.SemaphoreType.DMA,
            pltpu.SemaphoreType.DMA((2 * (tokens // block) + 2,)),
        ],
        compiler_params=pltpu.CompilerParams(vmem_limit_bytes=32 * MIB),
        name="basis",
    )(m, sketch_t, in_hbm(keys))


def spread(x, axis):
    n = lax.axis_size(axis)
    return lax.all_to_all(jnp.broadcast_to(x[None], (n,) + x.shape), axis, 0, 0)


def sum_over_seq(m):
    part = lax.all_to_all(m, "inner", 0, 0).sum(0)
    part = spread(part, "outer").sum(0)
    return spread(part, "inner")


def body(keys, sketch):
    total_tokens = keys.shape[0] * lax.axis_size("outer") * lax.axis_size("inner")
    m = sum_over_seq(moments(keys, sketch.T))
    basis_t, coefficients = finish(m, sketch.T, keys, total_tokens)
    return basis_t.T, coefficients


def solution(mesh):
    seq, head = mesh.shape["seq"], mesh.shape["head"]
    devices = mesh.devices.reshape(seq // INNER, INNER, head)
    return jax.shard_map(
        body,
        mesh=Mesh(devices, ("outer", "inner", "head")),
        in_specs=(P(("outer", "inner"), "head"), P()),
        out_specs=(P(("outer", "inner"), "head"), P("head", None)),
        check_vma=False,
    )
```

```python
import functools

import jax
import jax.numpy as jnp
from jax import lax
from jax.experimental import pallas as pl
from jax.experimental.pallas import tpu as pltpu
from jax.sharding import Mesh, PartitionSpec as P

INNER = 16
ROWS_OUT, COLS_OUT = 40, 128
AHEAD = 0
FIRST = 3
F32, BF16 = jnp.float32, jnp.bfloat16
MIB = 1 << 20


def dot(a, b, ca, cb):
    return lax.dot_general(a, b, (((ca,), (cb,)), ((), ())), preferred_element_type=F32)


def split3(x):
    a = x.astype(BF16)
    rest = x - a.astype(F32)
    b = rest.astype(BF16)
    return a, b, (rest - b.astype(F32)).astype(BF16)


def moments_kernel(block, k_hbm, st_hbm, m_ref, keys, st_ref, sem, st_sem):
    tokens, cols = keys.shape
    h = cols // 2
    copies = []
    for i in range(tokens // block):
        rows = pl.ds(i * block, block)
        copies.append(pltpu.make_async_copy(k_hbm.at[rows, :], keys.at[rows, :], sem.at[i]))
        copies[-1].start()
    st_copy = pltpu.make_async_copy(st_hbm, st_ref, st_sem)
    st_copy.start()
    top = jnp.zeros((h, cols), F32)
    low = jnp.zeros((h, h), F32)
    for i, copy in enumerate(copies):
        copy.wait()
        x = keys[i * block : (i + 1) * block, :]
        r = x[:, h:]
        top += dot(x[:, :h], x, 0, 0)
        low += jnp.concatenate([dot(r[:, : h // 2], r, 0, 0), dot(r[:, h // 2 :], r, 0, 0)], axis=0)
    st_copy.wait()
    st = st_ref[...]
    tops, lows = split3(top)[::-1], split3(low)[::-1]
    first = jnp.concatenate([st[:, :h]] * 3, axis=1)
    second = jnp.concatenate([st[:, h:]] * 3, axis=1)
    corner = jnp.concatenate([x[:, :h] for x in tops], axis=0)
    upper = jnp.concatenate([x[:, h:] for x in tops], axis=0)
    lower_t = jnp.concatenate([x[:, h:] for x in tops], axis=1)
    left = dot(first, corner, 1, 0) + dot(second, lower_t, 1, 1)
    right = dot(first, upper, 1, 0) + dot(second, jnp.concatenate(lows, axis=0), 1, 0)
    put_chunks(m_ref, jnp.concatenate([left, right], axis=1))


def put_chunks(ref, m):
    wide = m.shape[1] // COLS_OUT
    for i in range(ref.shape[0]):
        r, c = i // wide * ROWS_OUT, i % wide * COLS_OUT
        ref[i] = m[r : r + ROWS_OUT, c : c + COLS_OUT]


def in_hbm(x):
    return pltpu.with_memory_space_constraint(x, pltpu.HBM)


def moments(keys, sketch_t, block=768):
    tokens, cols = keys.shape
    rank = sketch_t.shape[0]
    chunks = (rank // ROWS_OUT) * (cols // COLS_OUT)
    vmem = pl.BlockSpec(memory_space=pltpu.VMEM)
    return pl.pallas_call(
        functools.partial(moments_kernel, block),
        out_shape=jax.ShapeDtypeStruct((chunks, ROWS_OUT, COLS_OUT), F32),
        in_specs=[pl.BlockSpec(memory_space=pltpu.HBM)] * 2,
        out_specs=vmem,
        scratch_shapes=[
            pltpu.VMEM((tokens, cols), BF16),
            pltpu.VMEM((rank, cols), BF16),
            pltpu.SemaphoreType.DMA((tokens // block,)),
            pltpu.SemaphoreType.DMA,
        ],
        compiler_params=pltpu.CompilerParams(vmem_limit_bytes=24 * MIB),
        name="moments",
    )(in_hbm(keys), in_hbm(sketch_t))


def lanes_of(tile, j):
    return jnp.broadcast_to(tile[:, j : j + 1], (8, 128))


def row_of(tile, s):
    return jnp.broadcast_to(tile[s : s + 1, :], (8, 128))


def invert_factor(t, per=2, panel=2, beside=lambda block, t: None):
    n, wide, width = len(t), len(t[0]), 8 * per
    sub = lax.broadcasted_iota(jnp.int32, (8, 128), 0)
    lane = lax.broadcasted_iota(jnp.int32, (8, 128), 1)

    def above(b, p):
        return p if b + per == n else 0

    for b in range(0, n, per):
        at, off = 8 * b // 128, 8 * b % 128
        cols = [[lanes_of(t[b + r][at], off + s) for r in range(per)] for s in range(width)]
        solved = [list(t[b + r]) for r in range(per)]
        factor = [list(t[b + r]) for r in range(per)]
        for s in range(width):
            p, q = divmod(s, 8)
            here = sub == q
            pivot = row_of(cols[s][p], q)
            inv, root = 1.0 / pivot, lax.rsqrt(pivot)
            for h in range(wide):
                row, olds = row_of(solved[p][h], q), [solved[r][h] for r in range(per)]
                if h == at:
                    row = jnp.where(lane == off + s, 1.0, row)
                    olds = [jnp.where(lane == off + s, 0.0, x) for x in olds]
                factor[p][h] = jnp.where(here, row * root, factor[p][h])
                row = row * inv
                for r in range(above(b, p), per):
                    x = olds[r] - cols[s][r] * row
                    solved[r][h] = jnp.where(here, row, x) if r == p else x
            for k in range(s + 1, width):
                val = row_of(cols[k][p], q) * inv
                for r in range(above(b, p), per):
                    x = cols[k][r] - cols[s][r] * val
                    cols[k][r] = jnp.where(here, val, x) if r == p else x
        in_block = (lane >= off) & (lane < off + width)
        end, far = (b // panel + 1) * panel, min(n, (b // panel + 2) * panel)
        for i in range(b + per, far):
            left = [lanes_of(t[i][at], off + s) for s in range(width)]
            for h in range(wide):
                x = jnp.where(in_block, 0.0, t[i][h]) if h == at else t[i][h]
                parts = [left[s] * row_of(solved[s // 8][h], s % 8) for s in range(width)]
                while len(parts) > 1:
                    parts = [p + q for p, q in zip(parts[::2], parts[1::2])]
                t[i][h] = x - parts[0]
        for r in range(per):
            t[b + r] = factor[r]
        beside(b // per, t)
        if b + per == end and far < n:
            rows = range(end - panel, end)
            u = jnp.concatenate(
                [
                    jnp.concatenate(
                        [
                            jnp.where((lane + 128 * h > sub + 8 * i) & (lane + 128 * h < 8 * end), 0.0, t[i][h])
                            for h in range(wide)
                        ],
                        axis=1,
                    )
                    for i in rows
                ],
                axis=0,
            )
            a1, a2, a3 = split3(u)
            skip = 8 * far // 128 * 128
            out = dot(
                jnp.concatenate([a3, a1, a2, a2, a1, a1], axis=0)[:, skip:],
                jnp.concatenate([a1, a3, a2, a1, a2, a1], axis=0),
                0,
                0,
            )
            for i in range(far, n):
                for h in range(wide):
                    done = (lane + 128 * h >= 8 * (end - panel)) & (lane + 128 * h < 8 * end)
                    x = jnp.where(done, 0.0, t[i][h])
                    t[i][h] = x - out[8 * i - skip : 8 * i + 8 - skip, 128 * h : 128 * h + 128]
    return t


def basis_kernel(
    scale, block, m_ref, st_any, k_hbm, qt_hbm, c_hbm, st_ref, keys, s_high, s_low, out, coef, tri, first_sem, in_sem, out_sem
):
    tokens, cols = keys.shape
    rank = st_ref.shape[0]
    steps = tokens // block
    st_copy = pltpu.make_async_copy(st_any, st_ref, first_sem)
    st_copy.start()
    load = pltpu.make_async_copy(k_hbm, keys, in_sem)
    load.start()
    wide = cols // COLS_OUT
    m = jnp.concatenate(
        [
            jnp.concatenate([m_ref[r * wide + c] for c in range(wide)], axis=1)
            for r in range(rank // ROWS_OUT)
        ],
        axis=0,
    )
    pieces = split3(m)
    st_copy.wait()
    st = st_ref[...]
    three = dot(jnp.concatenate(pieces, axis=0), st, 1, 1)
    gram = (three[2 * rank :] + three[rank : 2 * rank]) + three[:rank]
    tri[...] = jnp.zeros_like(tri)
    tri[:, :rank] = gram
    n, lanes = rank // 8, tri.shape[1] // 128
    t = [
        [tri[8 * i : 8 * i + 8, 128 * h : 128 * h + 128] for h in range(lanes)]
        for i in range(n)
    ]

    def halves(x):
        high = x.astype(BF16)
        return high, (x - high.astype(F32)).astype(BF16)

    def lower(i, h):
        sub = lax.broadcasted_iota(jnp.int32, (8, 128), 0)
        lane = lax.broadcasted_iota(jnp.int32, (8, 128), 1)
        return jnp.where(lane + 128 * h <= sub + 8 * i, t[i][h], 0.0)

    copies = []

    def send(first, last, rows):
        piece = (pl.ds(first, last - first), rows)
        copies.append(pltpu.make_async_copy(out.at[piece], qt_hbm.at[piece], out_sem.at[len(copies)]))
        copies[-1].start()

    def basis_rows(first, last, x, chunk):
        depth, count = x.shape[1], last - first
        high, low = halves(scale * x)
        rows = pl.ds(chunk * block, block)
        y = dot(jnp.concatenate([high, low], axis=0), s_high[:depth, rows], 1, 0)
        y = y[:count] + (y[count:] + dot(high, s_low[:depth, rows], 1, 0))
        out[first:last, rows] = y.astype(BF16)
        send(first, last, rows)

    def coefficient_rows(first, last, x):
        depth = x.shape[1]
        high, low = halves(x)
        p = [piece[:depth] for piece in pieces[:2]]
        coef[first:last, :] = dot(high, p[1], 1, 0) + dot(low, p[0], 1, 0) + dot(high, p[0], 1, 0)
        piece = (pl.ds(first, last - first), slice(None))
        copies.append(pltpu.make_async_copy(coef.at[piece], c_hbm.at[piece], out_sem.at[len(copies)]))
        copies[-1].start()

    early = rank // 128 * 128
    ready = early // 16 - 1

    def beside(step, t):
        if step == FIRST:
            load.wait()
        i = step - FIRST
        if 0 <= i < steps:
            rows = pl.ds(i * block, block)
            y = dot(st, keys[rows, :], 1, 1)
            s_high[:, rows], s_low[:, rows] = halves(y)
        if step >= ready:
            x = jnp.concatenate(
                [jnp.concatenate([lower(i, h) for h in range(early // 128)], axis=1) for i in range(early // 8)],
                axis=0,
            )
            for chunk in range(steps):
                if (chunk < AHEAD) == (step == ready) and step <= ready + 1:
                    basis_rows(0, early, x, chunk)
            if step == ready + 1:
                coefficient_rows(0, early, x)

    t = invert_factor(t, beside=beside)
    for i in range(early // 8, n):
        for h in range(lanes):
            tri[8 * i : 8 * i + 8, 128 * h : 128 * h + 128] = lower(i, h)
    x = tri[early:, :rank]
    coefficient_rows(early, rank, x)
    for chunk in range(steps):
        basis_rows(early, rank, x, chunk)
    for copy in copies:
        copy.wait()


def finish(m, sketch_t, keys, total_tokens, block=1024):
    tokens, cols = keys.shape
    rank = sketch_t.shape[0]
    anywhere = pl.BlockSpec(memory_space=pl.ANY)
    hbm = pl.BlockSpec(memory_space=pltpu.HBM)
    return pl.pallas_call(
        functools.partial(basis_kernel, float(total_tokens) ** 0.5, block),
        out_shape=(
            jax.ShapeDtypeStruct((rank, tokens), BF16),
            jax.ShapeDtypeStruct((rank, cols), F32),
        ),
        in_specs=[pl.BlockSpec(memory_space=pltpu.VMEM), anywhere, hbm],
        out_specs=(hbm, hbm),
        scratch_shapes=[
            pltpu.VMEM((rank, cols), BF16),
            pltpu.VMEM((tokens, cols), BF16),
            pltpu.VMEM((rank, tokens), BF16),
            pltpu.VMEM((rank, tokens), BF16),
            pltpu.VMEM((rank, tokens), BF16),
            pltpu.VMEM((rank, cols), F32),
            pltpu.VMEM((rank, -(-rank // 128) * 128), F32),
            pltpu.SemaphoreType.DMA,
            pltpu.SemaphoreType.DMA,
            pltpu.SemaphoreType.DMA((2 * (tokens // block) + 2,)),
        ],
        compiler_params=pltpu.CompilerParams(vmem_limit_bytes=32 * MIB),
        name="basis",
    )(m, sketch_t, in_hbm(keys))


def spread(x, axis):
    n = lax.axis_size(axis)
    return lax.all_to_all(jnp.broadcast_to(x[None], (n,) + x.shape), axis, 0, 0)


def sum_over_seq(m):
    part = lax.all_to_all(m, "inner", 0, 0).sum(0)
    part = spread(part, "outer").sum(0)
    return spread(part, "inner")


def body(keys, sketch):
    total_tokens = keys.shape[0] * lax.axis_size("outer") * lax.axis_size("inner")
    m = sum_over_seq(moments(keys, sketch.T))
    basis_t, coefficients = finish(m, sketch.T, keys, total_tokens)
    return basis_t.T, coefficients


def solution(mesh):
    seq, head = mesh.shape["seq"], mesh.shape["head"]
    devices = mesh.devices.reshape(seq // INNER, INNER, head)
    return jax.shard_map(
        body,
        mesh=Mesh(devices, ("outer", "inner", "head")),
        in_specs=(P(("outer", "inner"), "head"), P()),
        out_specs=(P(("outer", "inner"), "head"), P("head", None)),
        check_vma=False,
    )
```

```python
import functools

import jax
import jax.numpy as jnp
from jax import lax
from jax.experimental import pallas as pl
from jax.experimental.pallas import tpu as pltpu
from jax.sharding import Mesh, PartitionSpec as P

INNER = 16
ROWS_OUT, COLS_OUT = 40, 128
AHEAD = 0
FIRST = 3
F32, BF16 = jnp.float32, jnp.bfloat16
MIB = 1 << 20


def dot(a, b, ca, cb):
    return lax.dot_general(a, b, (((ca,), (cb,)), ((), ())), preferred_element_type=F32)


def split3(x):
    a = x.astype(BF16)
    rest = x - a.astype(F32)
    b = rest.astype(BF16)
    return a, b, (rest - b.astype(F32)).astype(BF16)


def moments_kernel(block, k_hbm, st_hbm, m_ref, keys, st_ref, sem, st_sem):
    tokens, cols = keys.shape
    h = cols // 2
    copies = []
    for i in range(tokens // block):
        rows = pl.ds(i * block, block)
        copies.append(pltpu.make_async_copy(k_hbm.at[rows, :], keys.at[rows, :], sem.at[i]))
        copies[-1].start()
    st_copy = pltpu.make_async_copy(st_hbm, st_ref, st_sem)
    st_copy.start()
    top = jnp.zeros((h, cols), F32)
    low = jnp.zeros((h, h), F32)
    for i, copy in enumerate(copies):
        copy.wait()
        x = keys[i * block : (i + 1) * block, :]
        r = x[:, h:]
        top += dot(x[:, :h], x, 0, 0)
        low += jnp.concatenate([dot(r[:, : h // 2], r, 0, 0), dot(r[:, h // 2 :], r, 0, 0)], axis=0)
    st_copy.wait()
    st = st_ref[...]
    tops, lows = split3(top)[::-1], split3(low)[::-1]
    first = jnp.concatenate([st[:, :h]] * 3, axis=1)
    second = jnp.concatenate([st[:, h:]] * 3, axis=1)
    corner = jnp.concatenate([x[:, :h] for x in tops], axis=0)
    upper = jnp.concatenate([x[:, h:] for x in tops], axis=0)
    lower_t = jnp.concatenate([x[:, h:] for x in tops], axis=1)
    left = dot(first, corner, 1, 0) + dot(second, lower_t, 1, 1)
    right = dot(first, upper, 1, 0) + dot(second, jnp.concatenate(lows, axis=0), 1, 0)
    put_chunks(m_ref, jnp.concatenate([left, right], axis=1))


def put_chunks(ref, m):
    wide = m.shape[1] // COLS_OUT
    for i in range(ref.shape[0]):
        r, c = i // wide * ROWS_OUT, i % wide * COLS_OUT
        ref[i] = m[r : r + ROWS_OUT, c : c + COLS_OUT]


def in_hbm(x):
    return pltpu.with_memory_space_constraint(x, pltpu.HBM)


def moments(keys, sketch_t, block=768):
    tokens, cols = keys.shape
    rank = sketch_t.shape[0]
    chunks = (rank // ROWS_OUT) * (cols // COLS_OUT)
    vmem = pl.BlockSpec(memory_space=pltpu.VMEM)
    return pl.pallas_call(
        functools.partial(moments_kernel, block),
        out_shape=jax.ShapeDtypeStruct((chunks, ROWS_OUT, COLS_OUT), F32),
        in_specs=[pl.BlockSpec(memory_space=pltpu.HBM)] * 2,
        out_specs=vmem,
        scratch_shapes=[
            pltpu.VMEM((tokens, cols), BF16),
            pltpu.VMEM((rank, cols), BF16),
            pltpu.SemaphoreType.DMA((tokens // block,)),
            pltpu.SemaphoreType.DMA,
        ],
        compiler_params=pltpu.CompilerParams(vmem_limit_bytes=24 * MIB),
        name="moments",
    )(in_hbm(keys), in_hbm(sketch_t))


def lanes_of(tile, j):
    return jnp.broadcast_to(tile[:, j : j + 1], (8, 128))


def row_of(tile, s):
    return jnp.broadcast_to(tile[s : s + 1, :], (8, 128))


def invert_factor(t, per=2, panel=2, beside=lambda block, t: None):
    n, wide, width = len(t), len(t[0]), 8 * per
    sub = lax.broadcasted_iota(jnp.int32, (8, 128), 0)
    lane = lax.broadcasted_iota(jnp.int32, (8, 128), 1)

    def above(b, p):
        return p if b + per == n else 0

    for b in range(0, n, per):
        at, off = 8 * b // 128, 8 * b % 128
        cols = [[lanes_of(t[b + r][at], off + s) for r in range(per)] for s in range(width)]
        solved = [list(t[b + r]) for r in range(per)]
        factor = [list(t[b + r]) for r in range(per)]
        for s in range(width):
            p, q = divmod(s, 8)
            here = sub == q
            pivot = following if s else row_of(cols[s][p], q)
            inv, root = 1.0 / pivot, lax.rsqrt(pivot)
            if s + 1 < width:
                p1, q1 = divmod(s + 1, 8)
                following = row_of(cols[s + 1][p1], q1) - (row_of(cols[s][p1], q1) * inv) * row_of(cols[s + 1][p], q)
            for h in range(wide):
                row, olds = row_of(solved[p][h], q), [solved[r][h] for r in range(per)]
                if h == at:
                    row = jnp.where(lane == off + s, 1.0, row)
                    olds = [jnp.where(lane == off + s, 0.0, x) for x in olds]
                factor[p][h] = jnp.where(here, row * root, factor[p][h])
                row = row * inv
                for r in range(above(b, p), per):
                    x = olds[r] - cols[s][r] * row
                    solved[r][h] = jnp.where(here, row, x) if r == p else x
            for k in range(s + 1, width):
                val = row_of(cols[k][p], q) * inv
                for r in range(above(b, p), per):
                    x = cols[k][r] - cols[s][r] * val
                    cols[k][r] = jnp.where(here, val, x) if r == p else x
        in_block = (lane >= off) & (lane < off + width)
        end, far = (b // panel + 1) * panel, min(n, (b // panel + 2) * panel)
        for i in range(b + per, far):
            left = [lanes_of(t[i][at], off + s) for s in range(width)]
            for h in range(wide):
                x = jnp.where(in_block, 0.0, t[i][h]) if h == at else t[i][h]
                parts = [left[s] * row_of(solved[s // 8][h], s % 8) for s in range(width)]
                while len(parts) > 1:
                    parts = [p + q for p, q in zip(parts[::2], parts[1::2])]
                t[i][h] = x - parts[0]
        for r in range(per):
            t[b + r] = factor[r]
        beside(b // per, t)
        if b + per == end and far < n:
            rows = range(end - panel, end)
            u = jnp.concatenate(
                [
                    jnp.concatenate(
                        [
                            jnp.where((lane + 128 * h > sub + 8 * i) & (lane + 128 * h < 8 * end), 0.0, t[i][h])
                            for h in range(wide)
                        ],
                        axis=1,
                    )
                    for i in rows
                ],
                axis=0,
            )
            a1, a2, a3 = split3(u)
            skip = 8 * far // 128 * 128
            out = dot(
                jnp.concatenate([a3, a1, a2, a2, a1, a1], axis=0)[:, skip:],
                jnp.concatenate([a1, a3, a2, a1, a2, a1], axis=0),
                0,
                0,
            )
            for i in range(far, n):
                for h in range(wide):
                    done = (lane + 128 * h >= 8 * (end - panel)) & (lane + 128 * h < 8 * end)
                    x = jnp.where(done, 0.0, t[i][h])
                    t[i][h] = x - out[8 * i - skip : 8 * i + 8 - skip, 128 * h : 128 * h + 128]
    return t


def basis_kernel(
    scale, block, m_ref, st_any, k_hbm, qt_hbm, c_hbm, st_ref, keys, s_high, s_low, out, coef, tri, first_sem, in_sem, out_sem
):
    tokens, cols = keys.shape
    rank = st_ref.shape[0]
    steps = tokens // block
    st_copy = pltpu.make_async_copy(st_any, st_ref, first_sem)
    st_copy.start()
    load = pltpu.make_async_copy(k_hbm, keys, in_sem)
    load.start()
    wide = cols // COLS_OUT
    m = jnp.concatenate(
        [
            jnp.concatenate([m_ref[r * wide + c] for c in range(wide)], axis=1)
            for r in range(rank // ROWS_OUT)
        ],
        axis=0,
    )
    pieces = split3(m)
    st_copy.wait()
    st = st_ref[...]
    three = dot(jnp.concatenate(pieces, axis=0), st, 1, 1)
    gram = (three[2 * rank :] + three[rank : 2 * rank]) + three[:rank]
    tri[...] = jnp.zeros_like(tri)
    tri[:, :rank] = gram
    n, lanes = rank // 8, tri.shape[1] // 128
    t = [
        [tri[8 * i : 8 * i + 8, 128 * h : 128 * h + 128] for h in range(lanes)]
        for i in range(n)
    ]

    def halves(x):
        high = x.astype(BF16)
        return high, (x - high.astype(F32)).astype(BF16)

    def lower(i, h):
        sub = lax.broadcasted_iota(jnp.int32, (8, 128), 0)
        lane = lax.broadcasted_iota(jnp.int32, (8, 128), 1)
        return jnp.where(lane + 128 * h <= sub + 8 * i, t[i][h], 0.0)

    copies = []

    def send(first, last, rows):
        piece = (pl.ds(first, last - first), rows)
        copies.append(pltpu.make_async_copy(out.at[piece], qt_hbm.at[piece], out_sem.at[len(copies)]))
        copies[-1].start()

    def basis_rows(first, last, x, chunk):
        depth, count = x.shape[1], last - first
        high, low = halves(scale * x)
        rows = pl.ds(chunk * block, block)
        y = dot(jnp.concatenate([high, low], axis=0), s_high[:depth, rows], 1, 0)
        y = y[:count] + (y[count:] + dot(high, s_low[:depth, rows], 1, 0))
        out[first:last, rows] = y.astype(BF16)
        send(first, last, rows)

    def coefficient_rows(first, last, x):
        depth = x.shape[1]
        high, low = halves(x)
        p = [piece[:depth] for piece in pieces[:2]]
        coef[first:last, :] = dot(high, p[1], 1, 0) + dot(low, p[0], 1, 0) + dot(high, p[0], 1, 0)
        piece = (pl.ds(first, last - first), slice(None))
        copies.append(pltpu.make_async_copy(coef.at[piece], c_hbm.at[piece], out_sem.at[len(copies)]))
        copies[-1].start()

    early = rank // 128 * 128
    ready = early // 16 - 1

    def beside(step, t):
        if step == FIRST:
            load.wait()
        i = step - FIRST
        if 0 <= i < steps:
            rows = pl.ds(i * block, block)
            y = dot(st, keys[rows, :], 1, 1)
            s_high[:, rows], s_low[:, rows] = halves(y)
        if step >= ready:
            x = jnp.concatenate(
                [jnp.concatenate([lower(i, h) for h in range(early // 128)], axis=1) for i in range(early // 8)],
                axis=0,
            )
            for chunk in range(steps):
                if (chunk < AHEAD) == (step == ready) and step <= ready + 1:
                    basis_rows(0, early, x, chunk)
            if step == ready + 1:
                coefficient_rows(0, early, x)

    t = invert_factor(t, beside=beside)
    for i in range(early // 8, n):
        for h in range(lanes):
            tri[8 * i : 8 * i + 8, 128 * h : 128 * h + 128] = lower(i, h)
    x = tri[early:, :rank]
    coefficient_rows(early, rank, x)
    for chunk in range(steps):
        basis_rows(early, rank, x, chunk)
    for copy in copies:
        copy.wait()


def finish(m, sketch_t, keys, total_tokens, block=1024):
    tokens, cols = keys.shape
    rank = sketch_t.shape[0]
    anywhere = pl.BlockSpec(memory_space=pl.ANY)
    hbm = pl.BlockSpec(memory_space=pltpu.HBM)
    return pl.pallas_call(
        functools.partial(basis_kernel, float(total_tokens) ** 0.5, block),
        out_shape=(
            jax.ShapeDtypeStruct((rank, tokens), BF16),
            jax.ShapeDtypeStruct((rank, cols), F32),
        ),
        in_specs=[pl.BlockSpec(memory_space=pltpu.VMEM), anywhere, hbm],
        out_specs=(hbm, hbm),
        scratch_shapes=[
            pltpu.VMEM((rank, cols), BF16),
            pltpu.VMEM((tokens, cols), BF16),
            pltpu.VMEM((rank, tokens), BF16),
            pltpu.VMEM((rank, tokens), BF16),
            pltpu.VMEM((rank, tokens), BF16),
            pltpu.VMEM((rank, cols), F32),
            pltpu.VMEM((rank, -(-rank // 128) * 128), F32),
            pltpu.SemaphoreType.DMA,
            pltpu.SemaphoreType.DMA,
            pltpu.SemaphoreType.DMA((2 * (tokens // block) + 2,)),
        ],
        compiler_params=pltpu.CompilerParams(vmem_limit_bytes=32 * MIB),
        name="basis",
    )(m, sketch_t, in_hbm(keys))


def spread(x, axis):
    n = lax.axis_size(axis)
    return lax.all_to_all(jnp.broadcast_to(x[None], (n,) + x.shape), axis, 0, 0)


def sum_over_seq(m):
    part = lax.all_to_all(m, "inner", 0, 0).sum(0)
    part = spread(part, "outer").sum(0)
    return spread(part, "inner")


def body(keys, sketch):
    total_tokens = keys.shape[0] * lax.axis_size("outer") * lax.axis_size("inner")
    m = sum_over_seq(moments(keys, sketch.T))
    basis_t, coefficients = finish(m, sketch.T, keys, total_tokens)
    return basis_t.T, coefficients


def solution(mesh):
    seq, head = mesh.shape["seq"], mesh.shape["head"]
    devices = mesh.devices.reshape(seq // INNER, INNER, head)
    return jax.shard_map(
        body,
        mesh=Mesh(devices, ("outer", "inner", "head")),
        in_specs=(P(("outer", "inner"), "head"), P()),
        out_specs=(P(("outer", "inner"), "head"), P("head", None)),
        check_vma=False,
    )
```
